512 devices in a mesh: depth: 64 (over y, z), dp: 8 (over x, core).
Axes of the slice: x: 4, y: 4, z: 16, core: 2. Of those that a mesh axis runs over, the one named last changes fastest.
Arguments:
- features: bfloat16 [8, 8, 16, 256], P('dp'), may hold values from -6 to 6
- weights: bfloat16 [128, 3, 3, 256, 256], P('depth'), may hold values from -0.125 to 0.125
- gains: float32 [64, 256], P('depth'), may hold values from 0.75 to 1.25
- cotangent: bfloat16 [8, 8, 16, 256], P('dp'), may hold values from -6 to 6
Outputs:
- starts: bfloat16 [64, 8, 8, 16, 256], P('depth', 'dp')
- adjoints: bfloat16 [64, 8, 8, 16, 256], P('depth', 'dp')
- weight_grads: bfloat16 [128, 3, 3, 256, 256], P('depth', None, None, 'dp')
The draws below stay inside these ranges and needn't reach their ends.
All inputs are finite; a program needn't handle non-finite values.
Results may differ from the reference program's by a relative error of at most 0.035.
The reference program's roundings to bfloat16 on the way count: a program that leaves them out, or rounds other values in their place, can miss the bound.
Values may be sent and summed in bfloat16 or wider, within the bound.
A program may use at most 64 MiB of HBM per device.

```python
import jax
import jax.numpy as jnp
from jax import lax

C = 256
HT = 8
WD = 16
L_DEV = 2
B_DEV = 1
BLOCKS = 64
LAYERS = 128
BATCH = 8
N_DP = 8


def block_levels(stream_key, shape, split, least, top_value):
    def one(position, shards_of):
        draws = jax.random.uniform(jax.random.fold_in(jax.random.fold_in(stream_key, 6), position), (shards_of,), jnp.float32, least / len(split), top_value / len(split))
        return jnp.repeat(jnp.exp(draws), shape[position] // shards_of).reshape((-1,) + (1,) * (len(shape) - position - 1))

    gain = one(*split[0])
    for cut in split[1:]:
        gain = gain * one(*cut)
    return gain


def gaussian(stream_key, dims, scale, most, cuts=(), held_as=jnp.bfloat16):
    drawn = jax.random.normal(stream_key, dims, jnp.float32) * scale
    if len(cuts) > 0:
        drawn = block_levels(stream_key, dims, cuts, -0.22, 0.18) * drawn
    return jnp.clip(drawn, min=-most, max=most).astype(held_as)


def setup_inputs(seed: int = 0) -> dict:
    seeds = jax.random.split(jax.random.key(seed), 5)
    features = gaussian(seeds[0], (BATCH, HT, WD, C), 1.0, 6.0, ((0, 8),))
    weights = gaussian(seeds[1], (LAYERS, 3, 3, C, C), (9 * C) ** -0.5, 0.125, ((0, 64),))
    gains = jnp.clip(1.0 + 0.05 * jax.random.normal(seeds[2], (BLOCKS, C), jnp.float32), 0.75, 1.25)
    cotangent = gaussian(seeds[3], (BATCH, HT, WD, C), 1.0, 6.0, ((0, 8),))
    return dict(features=features, weights=weights, gains=gains, cotangent=cotangent)


step_size = 0.15
dims_spec = ('NHWC', 'HWIO', 'NHWC')

def convolve(inputs, kernel):
    return lax.conv_general_dilated(inputs, kernel, (1, 1), 'SAME', dimension_numbers=dims_spec, preferred_element_type=jnp.float32)

def layer_apply(state, kernel):
    active = jnp.maximum(state, 0.0).astype(jnp.bfloat16)
    return state + step_size * convolve(active, kernel)

def block_forward(state, kernels):
    inputs = []
    for layer_index in range(kernels.shape[0]):
        inputs.append(state)
        state = layer_apply(state, kernels[layer_index])
    return (state, inputs)

def kernel_grad(active, scaled):
    height = active.shape[1]
    width = active.shape[2]
    channels = active.shape[3]
    padded = jnp.pad(active, ((0, 0), (1, 1), (1, 1), (0, 0)))
    flat = scaled.reshape(-1, scaled.shape[3])
    result = []
    for offset_a in range(3):
        line = []
        for offset_b in range(3):
            window = padded[:, offset_a:offset_a + height, offset_b:offset_b + width, :].reshape(-1, channels)
            line.append(jnp.dot(window.T, flat, preferred_element_type=jnp.float32))
        result.append(jnp.stack(line))
    return jnp.stack(result)

def block_backward(inputs, kernels, cotan, with_weights):
    grads = []
    for layer_index in reversed(range(len(inputs))):
        state = inputs[layer_index]
        kernel = kernels[layer_index]
        scaled = (step_size * cotan).astype(jnp.bfloat16)
        if with_weights:
            active = jnp.maximum(state, 0.0).astype(jnp.bfloat16)
            grads.append(kernel_grad(active, scaled))
        flipped = jnp.swapaxes(kernel[::-1, ::-1], 2, 3)
        spread = convolve(scaled, flipped)
        cotan = cotan + jnp.where(state > 0.0, spread, 0.0)
    return (cotan, grads[::-1])

def reference(features, weights, gains, cotangent):
    blocks = gains.shape[0]
    kernels = weights.reshape(blocks, L_DEV, 3, 3, C, C)
    start = features.astype(jnp.float32)
    ending = cotangent.astype(jnp.float32)
    scales = gains[:, None, None, None, :]

    def fine_ends(states):
        return lax.map(lambda pair: block_forward(pair[0], pair[1])[0], (states, kernels))

    def forward_chain(offsets):

        def advance(carry, item):
            return (item[0] * carry + item[1], carry)
        return lax.scan(advance, start, (gains, offsets))[1]
    states = jnp.broadcast_to(start, (blocks,) + start.shape)
    previous = states
    for sweep in range(2):
        previous = states
        offsets = fine_ends(states) - scales * states
        states = forward_chain(offsets)
    linear_at = previous

    def one_block(triple):
        inputs = block_forward(triple[0], triple[1])[1]
        return block_backward(inputs, triple[1], triple[2], False)[0]

    def backward_chain(offsets):

        def retreat(carry, item):
            return (item[0] * carry + item[1], carry)
        return lax.scan(retreat, ending, (gains, offsets), reverse=True)[1]
    ends = jnp.broadcast_to(ending, (blocks,) + ending.shape)
    offsets = jnp.zeros_like(ends)
    for sweep in range(2):
        offsets = lax.map(one_block, (linear_at, kernels, ends)) - scales * ends
        ends = backward_chain(offsets)
    adjoints = scales * ends + offsets

    def block_grads(triple):
        kern = triple[1]
        grouped_states = triple[0].reshape(N_DP, B_DEV, HT, WD, C)
        grouped_ends = triple[2].reshape(N_DP, B_DEV, HT, WD, C)

        def group_grad(pair):
            inputs = block_forward(pair[0], kern)[1]
            return jnp.stack(block_backward(inputs, kern, pair[1], True)[1]).astype(jnp.bfloat16)
        parts = lax.map(group_grad, (grouped_states, grouped_ends))
        return lax.optimization_barrier(jnp.sum(parts.astype(jnp.float32), axis=0)).astype(jnp.bfloat16)
    all_grads = lax.map(block_grads, (linear_at, kernels, ends))
    return (states.astype(jnp.bfloat16), adjoints.astype(jnp.bfloat16), all_grads.reshape(weights.shape))
```

```python
import functools

import jax
import jax.numpy as jnp
from jax import lax
from jax.experimental import pallas as pl
from jax.experimental.pallas import tpu as pltpu
from jax.sharding import PartitionSpec as P

F32, BF16 = jnp.float32, jnp.bfloat16
STEP = 0.15
HT, WD, C = 8, 16, 256
POS = HT * WD
TAPS = 9
NARROW = (False, True, True, True)


def kernel(ny, nz, nx, *refs):
    (x_ref, w_hbm, g_ref, ct_ref, st_ref, ad_ref, gr_ref) = refs[:7]
    (wf, wt, xch, cch, g2, gz, gy, buf, buf_s, u1s, u2s, dsc, at, atr, lhs, sg, gsend, grecv) = refs[7:25]
    snds, recvs, tots, sos, sts = (refs[25 + 4 * i : 29 + 4 * i] for i in range(5))
    (send_sem, recv_sem, w_sem) = refs[45:]

    depth, dp = lax.axis_index("depth"), lax.axis_index("dp")
    y, z = depth // nz, depth % nz
    xx, core = dp // 2, dp % 2
    rows = 2 * POS // nz
    per_half = nz // 2
    half = z // per_half
    cs = C // (2 * nx)

    def at_z(k):
        return (y * nz + k, dp)

    def at_y(k):
        return (k * nz + z, dp)

    def at_x(k):
        return (depth, k * 2 + core)

    sibling = (depth, xx * 2 + 1 - core)

    def over_z(body):
        def hop(i, _):
            body((z + nz // 2 + (1 - 2 * (i % 2)) * ((i + 1) // 2)) % nz)
            return 0

        lax.fori_loop(0, nz - 1, hop, 0)

    def over_y(body):
        for i in range(1, ny):
            body((y + i) % ny)

    def over_x(body):
        for i in range(1, nx):
            body((xx + i) % nx)

    def send(src, dst, index, device):
        pltpu.make_async_remote_copy(
            src_ref=src,
            dst_ref=dst,
            send_sem=send_sem.at[index],
            recv_sem=recv_sem.at[index],
            device_id=device,
            device_id_type=pl.DeviceIdType.MESH,
        ).start()

    def wait(ref, sem):
        pltpu.make_async_copy(ref, ref, sem).wait()

    barrier = pltpu.get_barrier_semaphore()

    def greet(device):
        pl.semaphore_signal(barrier, inc=1, device_id=device, device_id_type=pl.DeviceIdType.MESH)

    over_z(lambda k: greet(at_z(k)))
    over_y(lambda k: greet(at_y(k)))
    over_x(lambda k: greet(at_x(k)))
    greet(sibling)
    fetch = [pltpu.make_async_copy(w_hbm.at[i], wf.at[i], w_sem.at[i]) for i in range(2)]
    for copy in fetch:
        copy.start()

    gain = g_ref[...]
    for h in range(2):
        g2[h] = gain[:, 128 * h : 128 * h + 128]

    def chunked(dst, value):
        for k in range(nz):
            r, h = rows * (k % per_half), k // per_half
            dst[k] = value[r : r + rows, 128 * h : 128 * h + 128].astype(dst.dtype)

    x = x_ref[...].astype(F32)
    cot = ct_ref[...].astype(F32)
    chunked(xch, x)
    chunked(cch, cot)
    edge = jnp.zeros((WD, C), BF16)
    for b in (buf.at[0], buf.at[1], buf_s):
        for i in range(3):
            b[i, 0:WD] = edge
            b[i, POS + WD : POS + 2 * WD] = edge

    column = lax.broadcasted_iota(jnp.int32, (POS, C), 0) % WD

    def stage(b, value):
        b[0, WD : POS + WD] = jnp.where(column > 0, pltpu.roll(value, 1, 0), 0.0).astype(BF16)
        b[1, WD : POS + WD] = value.astype(BF16)
        b[2, WD : POS + WD] = jnp.where(column < WD - 1, pltpu.roll(value, POS - 1, 0), 0.0).astype(BF16)

    def conv(b, w, flip=False):
        total = None
        for t in range(TAPS):
            window = b[t % 3, WD * (t // 3) : WD * (t // 3) + POS]
            part = jnp.dot(window, w[8 - t if flip else t], preferred_element_type=F32)
            total = part if total is None else total + part
        return total

    def layer(b, u, w):
        stage(b, jnp.maximum(u, 0.0))
        return u + STEP * conv(b, w)

    def scan_order(reverse):
        return range(nz - 1, -1, -1) if reverse else range(nz)

    def offsets_out(p, offsets):
        chunked(snds[p], offsets)
        over_z(lambda k: send(snds[p].at[k], recvs[p].at[z], 3 * p, at_z(k)))
        recvs[p][z] = snds[p][z]

    def totals_out(p, reverse):
        wait(recvs[p].at[pl.ds(0, nz - 1)], recv_sem.at[3 * p])
        carry = None
        for k in scan_order(reverse):
            item = recvs[p][k].astype(F32)
            carry = item if carry is None else gz[k] * carry + item
        tots[p][y] = carry
        over_y(lambda k: send(tots[p].at[y], tots[p].at[y], 3 * p + 1, at_y(k)))

    def states_out(p, reverse, first):
        if ny > 1:
            wait(tots[p].at[pl.ds(0, ny - 1)], recv_sem.at[3 * p + 1])
        carry = first[z]
        for k in range(ny - 1, 0, -1) if reverse else range(ny - 1):
            reached = k > y if reverse else k < y
            carry = jnp.where(reached, gy[k] * carry + tots[p][k], carry)
        order = scan_order(reverse)
        for k in order:
            sos[p][k] = carry.astype(sos[p].dtype)
            if k != order[-1]:
                carry = gz[k] * carry + recvs[p][k].astype(F32)
        over_z(lambda k: send(sos[p].at[k], sts[p].at[z], 3 * p + 2, at_z(k)))
        sts[p][z] = sos[p][z]

    def states_in(p):
        wait(sts[p].at[pl.ds(0, nz - 1)], recv_sem.at[3 * p + 2])
        halves = []
        for h in range(2):
            halves.append(jnp.concatenate([sts[p][h * per_half + k] for k in range(per_half)], axis=0))
        return jnp.concatenate(halves, axis=1)

    fetch[0].wait()
    middle = layer(buf.at[0], x, wf.at[0])
    pl.semaphore_wait(barrier, (nz - 1) + (ny - 1) + (nx - 1) + 1)
    over_z(lambda k: send(g2.at[k // per_half], gz.at[z], 12, at_z(k)))
    gz[z] = g2[half]
    fetch[1].wait()
    final = layer(buf.at[1], middle, wf.at[1])
    offsets_out(0, final - gain * x)
    for i in range(2):

        def flip(t, _, i=i):
            wt[i, t] = wf[i, t].T
            return 0

        lax.fori_loop(0, TAPS, flip, 0)
    wait(gz.at[pl.ds(0, nz - 1)], recv_sem.at[12])
    product = gz[0]
    for k in range(1, nz):
        product = product * gz[k]
    gy[y] = product
    over_y(lambda k: send(gy.at[y], gy.at[y], 13, at_y(k)))
    totals_out(0, False)
    if ny > 1:
        wait(gy.at[pl.ds(0, ny - 1)], recv_sem.at[13])
    states_out(0, False, xch)
    u1 = states_in(0)

    def adjoint(e):
        stage(buf_s, (STEP * e).astype(BF16).astype(F32))
        e = e + jnp.where(u2s[...] > 0.0, conv(buf_s, wt.at[1], True), 0.0)
        stage(buf_s, (STEP * e).astype(BF16).astype(F32))
        return e + jnp.where(u1s[...] > 0.0, conv(buf_s, wt.at[0], True), 0.0)

    u1s[...] = u1
    u2s[...] = layer(buf.at[0], u1, wf.at[0])
    offsets_out(2, adjoint(cot) - gain * cot)
    u1, u2 = u1s[...], u2s[...]
    final = layer(buf.at[1], u2, wf.at[1])
    for i, u in enumerate((u1, u2)):
        turned = jnp.maximum(u, 0.0).T.astype(BF16)
        for k in range(nx):
            at[k, i] = turned[2 * cs * k : 2 * cs * (k + 1)]
    totals_out(2, True)
    over_x(lambda k: send(at.at[k], atr.at[xx], 14, at_x(k)))
    atr[xx] = at[xx]
    states_out(2, True, cch)
    chunked(snds[1], final - gain * u1)
    recvs[1][z] = snds[1][z]
    e1 = states_in(2).astype(F32)

    over_z(lambda k: send(snds[1].at[k], recvs[1].at[z], 3, at_z(k)))
    d = adjoint(e1) - gain * e1
    offsets_out(3, d)
    dsc[...] = d
    totals_out(1, False)
    wait(atr.at[pl.ds(0, nx - 1)], recv_sem.at[14])

    place = lax.broadcasted_iota(jnp.int32, (2 * cs, POS), 1)
    line, cell = place // WD, place % WD

    def windows(i, _):
        for k in range(nx):
            value = atr[k, i].astype(F32)
            for t in range(TAPS):
                down, right = t // 3 - 1, t % 3 - 1
                moved = value
                if t != 4:
                    ok = (line + down >= 0) & (line + down < HT) & (cell + right >= 0) & (cell + right < WD)
                    moved = jnp.where(ok, pltpu.roll(value, (-down * WD - right) % POS, 1), 0.0)
                moved = moved.astype(BF16)
                for c in range(2):
                    lhs[i, c, t, :, POS * k : POS * (k + 1)] = moved[cs * c : cs * (c + 1)]
        return 0

    lax.fori_loop(0, 2, windows, 0)
    totals_out(3, True)
    states_out(3, True, cch)
    e2 = states_in(3).astype(F32)

    def scaled_out(i, e):
        s = (STEP * e).astype(BF16)
        sg[i, xx] = s
        over_x(lambda k: send(sg.at[i, xx], sg.at[i, xx], 15 + i, at_x(k)))
        return s

    s = scaled_out(1, e2)
    stage(buf_s, s.astype(F32))
    scaled_out(0, e2 + jnp.where(u2s[...] > 0.0, conv(buf_s, wt.at[1], True), 0.0))
    states_out(1, False, xch)
    ad_ref[...] = (gain * e2 + dsc[...]).astype(BF16)

    def part(i, c):
        right = sg[i].reshape(nx * POS, C)
        return jnp.dot(lhs[i, c].reshape(TAPS * cs, nx * POS), right, preferred_element_type=F32)

    for i in (1, 0):
        wait(sg.at[i, pl.ds(0, nx - 1)], recv_sem.at[15 + i])
        gsend[i] = part(i, 1 - core).astype(BF16)
        send(gsend.at[i], grecv.at[i], 17 + i, sibling)
    mine = [part(i, core) for i in (0, 1)]
    st_ref[...] = states_in(1)
    for i in (1, 0):
        wait(grecv.at[i], recv_sem.at[17 + i])
        gr_ref[i] = (mine[i] + grecv[i].astype(F32)).astype(BF16)

    for p in range(4):
        wait(snds[p].at[pl.ds(0, nz - 1)], send_sem.at[3 * p])
        if ny > 1:
            wait(tots[p].at[pl.ds(0, ny - 1)], send_sem.at[3 * p + 1])
        wait(sos[p].at[pl.ds(0, nz - 1)], send_sem.at[3 * p + 2])
    wait(gz.at[pl.ds(0, nz - 1)], send_sem.at[12])
    if ny > 1:
        wait(gy.at[pl.ds(0, ny - 1)], send_sem.at[13])
    wait(atr.at[pl.ds(0, nx - 1)], send_sem.at[14])
    for i in range(2):
        wait(sg.at[i, pl.ds(0, nx - 1)], send_sem.at[15 + i])
        wait(grecv.at[i], send_sem.at[17 + i])


def program(mesh, ny, nz, nx):
    rows = 2 * POS // nz
    cs = C // (2 * nx)
    vmem = pltpu.VMEM
    widths = [BF16 if narrow else F32 for narrow in NARROW]
    scratch = [
        vmem((2, TAPS, C, C), BF16),
        vmem((2, TAPS, C, C), BF16),
        vmem((nz, rows, 128), F32),
        vmem((nz, rows, 128), F32),
        vmem((2, 1, 128), F32),
        vmem((nz, 1, 128), F32),
        vmem((ny, 1, 128), F32),
        vmem((2, 3, POS + 2 * WD, C), BF16),
        vmem((3, POS + 2 * WD, C), BF16),
        vmem((POS, C), F32),
        vmem((POS, C), F32),
        vmem((POS, C), F32),
        vmem((nx, 2, 2 * cs, POS), BF16),
        vmem((nx, 2, 2 * cs, POS), BF16),
        vmem((2, 2, TAPS, cs, nx * POS), BF16),
        vmem((2, nx, POS, C), BF16),
        vmem((2, TAPS * cs, C), BF16),
        vmem((2, TAPS * cs, C), BF16),
    ]
    chunks = [vmem((nz, rows, 128), width) for width in widths]
    scratch += chunks + chunks
    scratch += [vmem((ny, rows, 128), F32)] * 4
    scratch += chunks + chunks
    scratch += [pltpu.SemaphoreType.DMA((19,)), pltpu.SemaphoreType.DMA((19,)), pltpu.SemaphoreType.DMA((2,))]

    def per_device(features, weights, gains, cotangent):
        inside = pl.BlockSpec(memory_space=pltpu.VMEM)
        starts, adjoints, grads = pl.pallas_call(
            functools.partial(kernel, ny, nz, nx),
            out_shape=(
                jax.ShapeDtypeStruct((POS, C), BF16),
                jax.ShapeDtypeStruct((POS, C), BF16),
                jax.ShapeDtypeStruct((2, TAPS * cs, C), BF16),
            ),
            in_specs=[inside, pl.BlockSpec(memory_space=pl.ANY), inside, inside],
            out_specs=(inside, inside, inside),
            scratch_shapes=scratch,
            compiler_params=pltpu.CompilerParams(
                collective_id=0, has_side_effects=True, vmem_limit_bytes=48 * 1024 * 1024
            ),
        )(
            features.reshape(POS, C),
            weights.reshape(2, TAPS, C, C),
            gains,
            cotangent.reshape(POS, C),
        )
        return (
            starts.reshape(1, 1, HT, WD, C),
            adjoints.reshape(1, 1, HT, WD, C),
            grads.reshape(2, 3, 3, cs, C),
        )

    return jax.shard_map(
        per_device,
        mesh=mesh,
        in_specs=(
            P("dp", None, None, None),
            P("depth", None, None, None, None),
            P("depth", None),
            P("dp", None, None, None),
        ),
        out_specs=(
            P("depth", "dp", None, None, None),
            P("depth", "dp", None, None, None),
            P("depth", None, None, "dp", None),
        ),
        check_vma=False,
    )


def solution(mesh):
    return program(mesh, ny=4, nz=16, nx=4)
```

```python
import functools

import jax
import jax.numpy as jnp
from jax import lax
from jax.experimental import pallas as pl
from jax.experimental.pallas import tpu as pltpu
from jax.sharding import PartitionSpec as P

F32, BF16 = jnp.float32, jnp.bfloat16
STEP = 0.15
HT, WD, C = 8, 16, 256
POS = HT * WD
TAPS = 9
VMEM_BYTES = 54000 * 1024
WIDTH = (F32, BF16, BF16, BF16)
OWNERS = (1, 1, 2, 2)


def kernel(ny, nz, nx, *refs):
    (x_hbm, w_hbm, g_hbm, ct_hbm, st_ref, ad_ref, gr_ref) = refs[:7]
    (x_ref, g_ref, ct_ref, wf, wt, xch, cch, g2, gz, gy) = refs[7:17]
    (buf, buf_s, u1s, u2s, dsc, at, atr, act, lhs, sg, s1g, gsend, grecv) = refs[17:30]
    snds, recvs, tots, sos, sts = (refs[30 + 4 * i : 34 + 4 * i] for i in range(5))
    (send_sem, recv_sem, fetch_sem) = refs[50:]

    depth, dp = lax.axis_index("depth"), lax.axis_index("dp")
    y, z = depth // nz, depth % nz
    xx, core = dp // 2, dp % 2
    chunks = [nz // m for m in OWNERS]
    mine = [z % n for n in chunks]
    half = [2 * mine[p] // chunks[p] for p in range(4)]
    cs = C // (2 * nx)

    def at_z(k):
        return (y * nz + k, dp)

    def at_y(k):
        return (k * nz + z, dp)

    def at_x(k):
        return (depth, k * 2 + core)

    sibling = (depth, xx * 2 + 1 - core)

    def over_z(body, n=nz):
        def hop(i, _):
            body((z + nz + (1 - 2 * (i % 2)) * (n // 2 - (i + 1) // 2)) % nz)
            return 0

        lax.fori_loop(0, n - 1, hop, 0)

    def over_y(body):
        for i in range(1, ny):
            body((y + i) % ny)

    def over_x(body):
        for i in sorted(range(1, nx), key=lambda i: -min(i, nx - i)):
            body(i, (xx + i) % nx)

    def send(src, dst, index, device):
        pltpu.make_async_remote_copy(
            src_ref=src,
            dst_ref=dst,
            send_sem=send_sem.at[index],
            recv_sem=recv_sem.at[index],
            device_id=device,
            device_id_type=pl.DeviceIdType.MESH,
        ).start()

    def wait(ref, sem):
        pltpu.make_async_copy(ref, ref, sem).wait()

    barrier = pltpu.get_barrier_semaphore()

    def greet(device):
        pl.semaphore_signal(barrier, inc=1, device_id=device, device_id_type=pl.DeviceIdType.MESH)

    over_z(lambda k: greet(at_z(k)))
    over_y(lambda k: greet(at_y(k)))
    over_x(lambda i, k: greet(at_x(k)))
    greet(sibling)
    pairs = [(x_hbm, x_ref), (w_hbm.at[0], wf.at[0]), (g_hbm, g_ref), (w_hbm.at[1], wf.at[1]), (ct_hbm, ct_ref)]
    fetch = [pltpu.make_async_copy(a, b, fetch_sem.at[i]) for i, (a, b) in enumerate(pairs)]
    for copy in fetch:
        copy.start()

    def chunked(dst, value):
        n, rows = dst.shape[0], dst.shape[1]
        for k in range(n):
            r, h = rows * (k % (n // 2)), 2 * k // n
            dst[k] = value[r : r + rows, 128 * h : 128 * h + 128].astype(dst.dtype)

    edge = jnp.zeros((WD, C), BF16)
    for b in (buf.at[0], buf.at[1], buf_s):
        for i in range(3):
            b[i, 0:WD] = edge
            b[i, POS + WD : POS + 2 * WD] = edge

    column = lax.broadcasted_iota(jnp.int32, (POS, C), 0) % WD

    def stage(b, value):
        b[0, WD : POS + WD] = jnp.where(column > 0, pltpu.roll(value, 1, 0), 0.0).astype(BF16)
        b[1, WD : POS + WD] = value.astype(BF16)
        b[2, WD : POS + WD] = jnp.where(column < WD - 1, pltpu.roll(value, POS - 1, 0), 0.0).astype(BF16)

    def conv(b, w, flip=False):
        total = None
        for t in range(TAPS):
            window = b[t % 3, WD * (t // 3) : WD * (t // 3) + POS]
            part = jnp.dot(window, w[8 - t if flip else t], preferred_element_type=F32)
            total = part if total is None else total + part
        return total

    def layer(b, u, w):
        stage(b, jnp.maximum(u, 0.0))
        return u + STEP * conv(b, w)

    def scan_order(reverse):
        return range(nz - 1, -1, -1) if reverse else range(nz)

    def offsets_out(p):
        over_z(lambda k: send(snds[p].at[k % chunks[p]], recvs[p].at[z], 3 * p, at_z(k)))

    def totals_out(p, reverse):
        wait(recvs[p].at[pl.ds(0, nz - 1)], recv_sem.at[3 * p])
        carry = None
        for k in scan_order(reverse):
            item = recvs[p][k].astype(F32)
            carry = item if carry is None else gz[k, half[p]] * carry + item
        tots[p][y] = carry
        over_y(lambda k: send(tots[p].at[y], tots[p].at[y], 3 * p + 1, at_y(k)))

    def states_out(p, reverse, first):
        if ny > 1:
            wait(tots[p].at[pl.ds(0, ny - 1)], recv_sem.at[3 * p + 1])
        carry = first[mine[p]]
        for k in range(ny - 1, 0, -1) if reverse else range(ny - 1):
            reached = k > y if reverse else k < y
            carry = jnp.where(reached, gy[k, half[p]] * carry + tots[p][k], carry)
        order = scan_order(reverse)
        for k in order:
            sos[p][k] = carry.astype(sos[p].dtype)
            if k != order[-1]:
                carry = gz[k, half[p]] * carry + recvs[p][k].astype(F32)
        over_z(lambda k: send(sos[p].at[k], sts[p].at[mine[p]], 3 * p + 2, at_z(k)), chunks[p])
        sts[p][mine[p]] = sos[p][z]

    def states_in(p):
        n = chunks[p]
        wait(sts[p].at[pl.ds(0, n - 1)], recv_sem.at[3 * p + 2])
        halves = []
        for h in range(2):
            halves.append(jnp.concatenate([sts[p][h * (n // 2) + k] for k in range(n // 2)], axis=0))
        return jnp.concatenate(halves, axis=1)

    fetch[0].wait()
    x = x_ref[...].astype(F32)
    fetch[1].wait()
    middle = layer(buf.at[0], x, wf.at[0])
    fetch[2].wait()
    gain = g_ref[...]
    for h in range(2):
        g2[h] = gain[:, 128 * h : 128 * h + 128]
    fetch[3].wait()
    chunked(snds[0], layer(buf.at[1], middle, wf.at[1]) - gain * x)
    pl.semaphore_wait(barrier, (nz - 1) + (ny - 1) + (nx - 1) + 1)
    offsets_out(0)
    over_z(lambda k: send(g2, gz.at[z], 12, at_z(k)))
    recvs[0][z] = snds[0][mine[0]]
    gz[z] = g2[...]
    fetch[4].wait()
    cot = ct_ref[...].astype(F32)
    chunked(xch, x)
    chunked(cch, cot)
    for i in range(2):

        def flip(t, _, i=i):
            wt[i, t] = wf[i, t].T
            return 0

        lax.fori_loop(0, TAPS, flip, 0)
    wait(gz.at[pl.ds(0, nz - 1)], recv_sem.at[12])
    product = gz[0]
    for k in range(1, nz):
        product = product * gz[k]
    gy[y] = product
    over_y(lambda k: send(gy.at[y], gy.at[y], 13, at_y(k)))
    totals_out(0, False)
    if ny > 1:
        wait(gy.at[pl.ds(0, ny - 1)], recv_sem.at[13])
    states_out(0, False, xch)
    u1 = states_in(0)

    def adjoint(e):
        stage(buf_s, (STEP * e).astype(BF16).astype(F32))
        e = e + jnp.where(u2s[...] > 0.0, conv(buf_s, wt.at[1], True), 0.0)
        stage(buf_s, (STEP * e).astype(BF16).astype(F32))
        return e + jnp.where(u1s[...] > 0.0, conv(buf_s, wt.at[0], True), 0.0)

    u1s[...] = u1
    u2s[...] = layer(buf.at[0], u1, wf.at[0])
    chunked(snds[2], adjoint(cot) - gain * cot)
    offsets_out(2)
    recvs[2][z] = snds[2][mine[2]]
    u1, u2 = u1s[...], u2s[...]
    for i, u in enumerate((u1, u2)):
        active = jnp.maximum(u, 0.0)
        turned = active.T.astype(BF16)
        for k in range(nx):
            at[k, i] = turned[2 * cs * k : 2 * cs * (k + 1)]
    act[xx] = active.astype(BF16)
    over_x(lambda i, k: send(at.at[k], atr.at[xx], 14, at_x(k)))
    over_x(lambda i, k: send(act.at[xx], act.at[xx], 15, at_x(k)))
    atr[xx] = at[xx]
    chunked(snds[1], layer(buf.at[1], u2, wf.at[1]) - gain * u1)
    totals_out(2, True)
    recvs[1][z] = snds[1][mine[1]]
    states_out(2, True, cch)
    offsets_out(1)
    e1 = states_in(2).astype(F32)

    d = adjoint(e1) - gain * e1
    chunked(snds[3], d)
    offsets_out(3)
    recvs[3][z] = snds[3][mine[3]]
    dsc[...] = d
    if nx > 1:
        wait(atr.at[pl.ds(0, nx - 1)], recv_sem.at[14])
        wait(act.at[pl.ds(0, nx - 1)], recv_sem.at[15])

    place = lax.broadcasted_iota(jnp.int32, (2 * cs, POS), 1)
    line, cell = place // WD, place % WD

    def windows(i, _):
        for k in range(nx):
            value = atr[k, i].astype(F32)
            for t in range(TAPS):
                down, right = t // 3 - 1, t % 3 - 1
                moved = value
                if t != 4:
                    ok = (line + down >= 0) & (line + down < HT) & (cell + right >= 0) & (cell + right < WD)
                    moved = jnp.where(ok, pltpu.roll(value, (-down * WD - right) % POS, 1), 0.0)
                moved = moved.astype(BF16)
                for c in range(2):
                    lhs[i, c, t, :, POS * k : POS * (k + 1)] = moved[cs * c : cs * (c + 1)]
        return 0

    lax.fori_loop(0, 2, windows, 0)
    totals_out(1, False)
    totals_out(3, True)
    states_out(3, True, cch)
    states_out(1, False, xch)
    e2 = states_in(3).astype(F32)

    s = (STEP * e2).astype(BF16)
    sg[xx] = s
    over_x(lambda i, k: send(sg.at[xx], sg.at[xx], 16 + i, at_x(k)))
    stage(buf_s, s.astype(F32))
    spread = conv(buf_s, wt.at[1], True)
    s1g[xx] = (STEP * (e2 + jnp.where(u2s[...] > 0.0, spread, 0.0))).astype(BF16)
    ad_ref[...] = (gain * e2 + dsc[...]).astype(BF16)

    def part(i, c, right):
        return jnp.dot(lhs[i, c].reshape(TAPS * cs, nx * POS), right[...].reshape(nx * POS, C), preferred_element_type=F32)

    def part_out(i, right):
        gsend[i] = part(i, 1 - core, right).astype(BF16)
        send(gsend.at[i], grecv.at[i], 16 + nx + i, sibling)

    arrivals = sorted(range(1, nx), key=lambda i: min(i, nx - i))
    for i in arrivals:
        k = (xx + nx - i) % nx
        wait(sg.at[0], recv_sem.at[16 + i])
        if i == arrivals[-1]:
            part_out(1, sg)
        s = sg[k].astype(F32)
        stage(buf_s, s)
        spread = conv(buf_s, wt.at[1], True)
        s1g[k] = (s + STEP * jnp.where(act[k].astype(F32) > 0.0, spread, 0.0)).astype(BF16)
    if nx == 1:
        part_out(1, sg)
    part_out(0, s1g)
    sums = [part(0, core, s1g), part(1, core, sg)]
    st_ref[...] = states_in(1)
    for i in (1, 0):
        wait(grecv.at[i], recv_sem.at[16 + nx + i])
        gr_ref[i] = (sums[i] + grecv[i].astype(F32)).astype(BF16)

    for p in range(4):
        wait(recvs[p].at[pl.ds(0, nz - 1)], send_sem.at[3 * p])
        if ny > 1:
            wait(tots[p].at[pl.ds(0, ny - 1)], send_sem.at[3 * p + 1])
        wait(sts[p].at[pl.ds(0, chunks[p] - 1)], send_sem.at[3 * p + 2])
    wait(gz.at[pl.ds(0, nz - 1)], send_sem.at[12])
    if ny > 1:
        wait(gy.at[pl.ds(0, ny - 1)], send_sem.at[13])
    if nx > 1:
        wait(atr.at[pl.ds(0, nx - 1)], send_sem.at[14])
        wait(act.at[pl.ds(0, nx - 1)], send_sem.at[15])
    for i in range(1, nx):
        wait(sg.at[0], send_sem.at[16 + i])
    for i in range(2):
        wait(grecv.at[i], send_sem.at[16 + nx + i])


def program(mesh, ny, nz, nx):
    cs = C // (2 * nx)
    vmem = pltpu.VMEM

    def states(m, width):
        return vmem((nz // m, 2 * POS * m // nz, 128), width)

    scratch = [
        vmem((POS, C), BF16),
        vmem((1, C), F32),
        vmem((POS, C), BF16),
        vmem((2, TAPS, C, C), BF16),
        vmem((2, TAPS, C, C), BF16),
        states(1, F32),
        states(2, F32),
        vmem((2, 1, 128), F32),
        vmem((nz, 2, 1, 128), F32),
        vmem((ny, 2, 1, 128), F32),
        vmem((2, 3, POS + 2 * WD, C), BF16),
        vmem((3, POS + 2 * WD, C), BF16),
        vmem((POS, C), F32),
        vmem((POS, C), F32),
        vmem((POS, C), F32),
        vmem((nx, 2, 2 * cs, POS), BF16),
        vmem((nx, 2, 2 * cs, POS), BF16),
        vmem((nx, POS, C), BF16),
        vmem((2, 2, TAPS, cs, nx * POS), BF16),
        vmem((nx, POS, C), BF16),
        vmem((nx, POS, C), BF16),
        vmem((2, TAPS * cs, C), BF16),
        vmem((2, TAPS * cs, C), BF16),
    ]
    kinds = list(zip(OWNERS, WIDTH))
    rows = [2 * POS * m // nz for m in OWNERS]
    scratch += [states(m, width) for m, width in kinds]
    scratch += [vmem((nz, r, 128), width) for r, width in zip(rows, WIDTH)]
    scratch += [vmem((ny, r, 128), F32) for r in rows]
    scratch += [vmem((nz, r, 128), width) for r, width in zip(rows, WIDTH)]
    scratch += [states(m, width) for m, width in kinds]
    sems = 18 + nx
    scratch += [pltpu.SemaphoreType.DMA((sems,)), pltpu.SemaphoreType.DMA((sems,)), pltpu.SemaphoreType.DMA((5,))]

    def per_device(features, weights, gains, cotangent):
        inside = pl.BlockSpec(memory_space=pltpu.VMEM)
        outside = pl.BlockSpec(memory_space=pltpu.HBM)
        shapes = (
            jax.ShapeDtypeStruct((POS, C), BF16),
            jax.ShapeDtypeStruct((POS, C), BF16),
            jax.ShapeDtypeStruct((2, TAPS * cs, C), BF16),
        )
        starts, adjoints, grads = pl.pallas_call(
            functools.partial(kernel, ny, nz, nx),
            out_shape=shapes,
            in_specs=[outside] * 4,
            out_specs=(inside,) * 3,
            scratch_shapes=scratch,
            compiler_params=pltpu.CompilerParams(
                collective_id=0, has_side_effects=True, vmem_limit_bytes=VMEM_BYTES
            ),
        )(
            features.reshape(POS, C),
            weights.reshape(2, TAPS, C, C),
            gains,
            cotangent.reshape(POS, C),
        )
        return (
            starts.reshape(1, 1, HT, WD, C),
            adjoints.reshape(1, 1, HT, WD, C),
            grads.reshape(2, 3, 3, cs, C),
        )

    return jax.shard_map(
        per_device,
        mesh=mesh,
        in_specs=(
            P("dp", None, None, None),
            P("depth", None, None, None, None),
            P("depth", None),
            P("dp", None, None, None),
        ),
        out_specs=(
            P("depth", "dp", None, None, None),
            P("depth", "dp", None, None, None),
            P("depth", None, None, "dp", None),
        ),
        check_vma=False,
    )


def solution(mesh):
    return program(mesh, ny=4, nz=16, nx=4)
```

```python
import functools

import jax
import jax.numpy as jnp
from jax import lax
from jax.experimental import pallas as pl
from jax.experimental.pallas import tpu as pltpu
from jax.sharding import PartitionSpec as P

F32, BF16 = jnp.float32, jnp.bfloat16
STEP = 0.15
HT, WD, C = 8, 16, 256
POS = HT * WD
TAPS = 9
VMEM_BYTES = 54000 * 1024
WIDTH = (BF16, BF16, BF16, BF16)
OWNERS = (2, 1, 2, 2)


def kernel(ny, nz, nx, *refs):
    (in_ref, w_hbm, st_ref, ad_ref, gr_ref) = refs[:5]
    (wf, wt, xch, xch2, cch, g2, gz, gy) = refs[5:13]
    (buf, buf_s, u1s, u2s, dsc, at, atr, act, lhs, sg, s1g, gsend, grecv) = refs[13:26]
    snds, recvs, tots, sos, sts = (refs[26 + 4 * i : 30 + 4 * i] for i in range(5))
    (send_sem, recv_sem, fetch_sem) = refs[46:]

    depth, dp = lax.axis_index("depth"), lax.axis_index("dp")
    y, z = depth // nz, depth % nz
    xx, core = dp // 2, dp % 2
    chunks = [nz // m for m in OWNERS]
    mine = [z % n for n in chunks]
    half = [2 * mine[p] // chunks[p] for p in range(4)]
    cs = C // (2 * nx)

    def at_z(k):
        return (y * nz + k, dp)

    def at_y(k):
        return (k * nz + z, dp)

    def at_x(k):
        return (depth, k * 2 + core)

    arrivals = sorted(range(1, nx), key=lambda i: min(i, nx - i))
    slot = {i: n + 1 for n, i in enumerate(arrivals)}
    sibling = (depth, xx * 2 + 1 - core)

    def over_z(body, n=nz):
        def hop(i, _):
            body((z + nz + (1 - 2 * (i % 2)) * (n // 2 - (i + 1) // 2)) % nz)
            return 0

        lax.fori_loop(0, n - 1, hop, 0)

    def over_y(body):
        for i in range(1, ny):
            body((y + i) % ny)

    def over_x(body):
        for i in reversed(arrivals):
            body(i, (xx + i) % nx)

    def send(src, dst, index, device):
        pltpu.make_async_remote_copy(
            src_ref=src,
            dst_ref=dst,
            send_sem=send_sem.at[index],
            recv_sem=recv_sem.at[index],
            device_id=device,
            device_id_type=pl.DeviceIdType.MESH,
        ).start()

    def wait(ref, sem):
        pltpu.make_async_copy(ref, ref, sem).wait()

    barrier = pltpu.get_barrier_semaphore()

    def greet(device):
        pl.semaphore_signal(barrier, inc=1, device_id=device, device_id_type=pl.DeviceIdType.MESH)

    over_z(lambda k: greet(at_z(k)))
    over_y(lambda k: greet(at_y(k)))
    over_x(lambda i, k: greet(at_x(k)))
    greet(sibling)
    fetch = [pltpu.make_async_copy(w_hbm.at[i], wf.at[i], fetch_sem.at[i]) for i in range(2)]
    for copy in fetch:
        copy.start()

    def chunked(dst, value):
        n, rows = dst.shape[0], dst.shape[1]
        for k in range(n):
            r, h = rows * (k % (n // 2)), 2 * k // n
            dst[k] = value[r : r + rows, 128 * h : 128 * h + 128].astype(dst.dtype)

    edge = jnp.zeros((WD, C), BF16)
    for b in (buf.at[0], buf.at[1], buf_s):
        for i in range(3):
            b[i, 0:WD] = edge
            b[i, POS + WD : POS + 2 * WD] = edge

    column = lax.broadcasted_iota(jnp.int32, (POS, C), 0) % WD

    def stage(b, value):
        b[0, WD : POS + WD] = jnp.where(column > 0, pltpu.roll(value, 1, 0), 0.0).astype(BF16)
        b[1, WD : POS + WD] = value.astype(BF16)
        b[2, WD : POS + WD] = jnp.where(column < WD - 1, pltpu.roll(value, POS - 1, 0), 0.0).astype(BF16)

    def conv(b, w, flip=False):
        total = None
        for t in range(TAPS):
            window = b[t % 3, WD * (t // 3) : WD * (t // 3) + POS]
            part = jnp.dot(window, w[8 - t if flip else t], preferred_element_type=F32)
            total = part if total is None else total + part
        return total

    def layer(b, u, w):
        stage(b, jnp.maximum(u, 0.0))
        return u + STEP * conv(b, w)

    def scan_order(reverse):
        return range(nz - 1, -1, -1) if reverse else range(nz)

    def offsets_out(p):
        over_z(lambda k: send(snds[p].at[k % chunks[p]], recvs[p].at[z], 3 * p, at_z(k)))

    def totals_out(p, reverse):
        wait(recvs[p].at[pl.ds(0, nz - 1)], recv_sem.at[3 * p])
        carry = None
        for k in scan_order(reverse):
            item = recvs[p][k].astype(F32)
            carry = item if carry is None else gz[k, half[p]] * carry + item
        tots[p][y] = carry
        over_y(lambda k: send(tots[p].at[y], tots[p].at[y], 3 * p + 1, at_y(k)))

    def states_out(p, reverse, first):
        if ny > 1:
            wait(tots[p].at[pl.ds(0, ny - 1)], recv_sem.at[3 * p + 1])
        carry = first[mine[p]]
        for k in range(ny - 1, 0, -1) if reverse else range(ny - 1):
            reached = k > y if reverse else k < y
            carry = jnp.where(reached, gy[k, half[p]] * carry + tots[p][k], carry)
        order = scan_order(reverse)
        for k in order:
            sos[p][k] = carry.astype(sos[p].dtype)
            if k != order[-1]:
                carry = gz[k, half[p]] * carry + recvs[p][k].astype(F32)
        over_z(lambda k: send(sos[p].at[k], sts[p].at[mine[p]], 3 * p + 2, at_z(k)), chunks[p])
        sts[p][mine[p]] = sos[p][z]

    def states_in(p):
        n = chunks[p]
        wait(sts[p].at[pl.ds(0, n - 1)], recv_sem.at[3 * p + 2])
        halves = []
        for h in range(2):
            halves.append(jnp.concatenate([sts[p][h * (n // 2) + k] for k in range(n // 2)], axis=0))
        return jnp.concatenate(halves, axis=1)

    x = in_ref[0:POS]
    cot = in_ref[POS : 2 * POS]
    gain = in_ref[2 * POS : 2 * POS + 1]
    fetch[0].wait()
    middle = layer(buf.at[0], x, wf.at[0])
    for h in range(2):
        g2[h] = gain[:, 128 * h : 128 * h + 128]
    fetch[1].wait()
    chunked(snds[0], layer(buf.at[1], middle, wf.at[1]) - gain * x)
    pl.semaphore_wait(barrier, (nz - 1) + (ny - 1) + (nx - 1) + 1)
    offsets_out(0)
    over_z(lambda k: send(g2, gz.at[z], 12, at_z(k)))
    recvs[0][z] = snds[0][mine[0]]
    gz[z] = g2[...]
    chunked(xch, x)
    chunked(xch2, x)
    chunked(cch, cot)
    for i in range(2):

        def flip(t, _, i=i):
            wt[i, t] = wf[i, t].T
            return 0

        lax.fori_loop(0, TAPS, flip, 0)
    wait(gz.at[pl.ds(0, nz - 1)], recv_sem.at[12])
    product = gz[0]
    for k in range(1, nz):
        product = product * gz[k]
    gy[y] = product
    over_y(lambda k: send(gy.at[y], gy.at[y], 13, at_y(k)))
    totals_out(0, False)
    if ny > 1:
        wait(gy.at[pl.ds(0, ny - 1)], recv_sem.at[13])
    states_out(0, False, xch2)
    u1 = states_in(0).astype(F32)

    def adjoint(e):
        stage(buf_s, (STEP * e).astype(BF16).astype(F32))
        e = e + jnp.where(u2s[...] > 0.0, conv(buf_s, wt.at[1], True), 0.0)
        stage(buf_s, (STEP * e).astype(BF16).astype(F32))
        return e + jnp.where(u1s[...] > 0.0, conv(buf_s, wt.at[0], True), 0.0)

    u1s[...] = u1
    u2s[...] = layer(buf.at[0], u1, wf.at[0])
    chunked(snds[2], adjoint(cot) - gain * cot)
    offsets_out(2)
    recvs[2][z] = snds[2][mine[2]]
    u1, u2 = u1s[...], u2s[...]
    for i, u in enumerate((u1, u2)):
        active = jnp.maximum(u, 0.0)
        turned = active.T.astype(BF16)
        for k in range(nx):
            at[k, i] = turned[2 * cs * k : 2 * cs * (k + 1)]
    act[0] = active.astype(BF16)
    over_x(lambda i, k: send(at.at[k], atr.at[slot[i]], 14, at_x(k)))
    over_x(lambda i, k: send(act.at[0], act.at[slot[i]], 15, at_x(k)))
    atr[0] = at[xx]
    chunked(snds[1], layer(buf.at[1], u2, wf.at[1]) - gain * u1)
    totals_out(2, True)
    recvs[1][z] = snds[1][mine[1]]
    states_out(2, True, cch)
    offsets_out(1)
    e1 = states_in(2).astype(F32)

    d = adjoint(e1) - gain * e1
    chunked(snds[3], d)
    offsets_out(3)
    recvs[3][z] = snds[3][mine[3]]
    dsc[...] = d
    if nx > 1:
        wait(atr.at[pl.ds(0, nx - 1)], recv_sem.at[14])
        wait(act.at[pl.ds(0, nx - 1)], recv_sem.at[15])

    place = lax.broadcasted_iota(jnp.int32, (2 * cs, POS), 1)
    line, cell = place // WD, place % WD

    def windows(i, _):
        for k in range(nx):
            value = atr[k, i].astype(F32)
            for t in range(TAPS):
                down, right = t // 3 - 1, t % 3 - 1
                moved = value
                if t != 4:
                    ok = (line + down >= 0) & (line + down < HT) & (cell + right >= 0) & (cell + right < WD)
                    moved = jnp.where(ok, pltpu.roll(value, (-down * WD - right) % POS, 1), 0.0)
                moved = moved.astype(BF16)
                for c in range(2):
                    lhs[i, c, t, :, POS * k : POS * (k + 1)] = moved[cs * c : cs * (c + 1)]
        return 0

    lax.fori_loop(0, 2, windows, 0)
    totals_out(1, False)
    totals_out(3, True)
    states_out(3, True, cch)
    states_out(1, False, xch)
    e2 = states_in(3).astype(F32)

    s = (STEP * e2).astype(BF16)
    sg[0] = s
    over_x(lambda i, k: send(sg.at[0], sg.at[slot[i]], 16 + i, at_x(k)))
    stage(buf_s, s.astype(F32))
    spread = conv(buf_s, wt.at[1], True)
    s1g[0] = (STEP * (e2 + jnp.where(u2s[...] > 0.0, spread, 0.0))).astype(BF16)
    ad_ref[...] = (gain * e2 + dsc[...]).astype(BF16)

    def part(i, c, first, last):
        count = last - first
        left = lhs[i, c, :, :, first * POS : last * POS].reshape(TAPS * cs, count * POS)
        right = (s1g, sg)[i][first:last].reshape(count * POS, C)
        return jnp.dot(left, right, preferred_element_type=F32)

    def below(i):
        s = sg[slot[i]].astype(F32)
        stage(buf_s, s)
        spread = conv(buf_s, wt.at[1], True)
        s1g[slot[i]] = (s + STEP * jnp.where(act[slot[i]].astype(F32) > 0.0, spread, 0.0)).astype(BF16)

    for i in arrivals[:-1]:
        wait(sg.at[0], recv_sem.at[16 + i])
        below(i)
    cores = (1 - core, core)
    early = [[part(i, c, 0, nx - 1) for c in cores] for i in range(2)]
    wait(sg.at[0], recv_sem.at[16 + arrivals[-1]])
    sums = [None, None]
    for i in (1, 0):
        if i == 0:
            below(arrivals[-1])
        gsend[i] = (early[i][0] + part(i, cores[0], nx - 1, nx)).astype(BF16)
        send(gsend.at[i], grecv.at[i], 16 + nx + i, sibling)
        sums[i] = early[i][1] + part(i, cores[1], nx - 1, nx)
    st_ref[...] = states_in(1)
    for i in (1, 0):
        wait(grecv.at[i], recv_sem.at[16 + nx + i])
        gr_ref[i] = (sums[i] + grecv[i].astype(F32)).astype(BF16)

    for p in range(4):
        wait(recvs[p].at[pl.ds(0, nz - 1)], send_sem.at[3 * p])
        if ny > 1:
            wait(tots[p].at[pl.ds(0, ny - 1)], send_sem.at[3 * p + 1])
        wait(sts[p].at[pl.ds(0, chunks[p] - 1)], send_sem.at[3 * p + 2])
    wait(gz.at[pl.ds(0, nz - 1)], send_sem.at[12])
    if ny > 1:
        wait(gy.at[pl.ds(0, ny - 1)], send_sem.at[13])
    if nx > 1:
        wait(atr.at[pl.ds(0, nx - 1)], send_sem.at[14])
        wait(act.at[pl.ds(0, nx - 1)], send_sem.at[15])
    for i in range(1, nx):
        wait(sg.at[0], send_sem.at[16 + i])
    for i in range(2):
        wait(grecv.at[i], send_sem.at[16 + nx + i])


def program(mesh, ny, nz, nx):
    cs = C // (2 * nx)
    vmem = pltpu.VMEM

    def states(m, width):
        return vmem((nz // m, 2 * POS * m // nz, 128), width)

    scratch = [
        vmem((2, TAPS, C, C), BF16),
        vmem((2, TAPS, C, C), BF16),
        states(1, F32),
        states(2, F32),
        states(2, F32),
        vmem((2, 1, 128), F32),
        vmem((nz, 2, 1, 128), F32),
        vmem((ny, 2, 1, 128), F32),
        vmem((2, 3, POS + 2 * WD, C), BF16),
        vmem((3, POS + 2 * WD, C), BF16),
        vmem((POS, C), F32),
        vmem((POS, C), F32),
        vmem((POS, C), F32),
        vmem((nx, 2, 2 * cs, POS), BF16),
        vmem((nx, 2, 2 * cs, POS), BF16),
        vmem((nx, POS, C), BF16),
        vmem((2, 2, TAPS, cs, nx * POS), BF16),
        vmem((nx, POS, C), BF16),
        vmem((nx, POS, C), BF16),
        vmem((2, TAPS * cs, C), BF16),
        vmem((2, TAPS * cs, C), BF16),
    ]
    kinds = list(zip(OWNERS, WIDTH))
    rows = [2 * POS * m // nz for m in OWNERS]
    scratch += [states(m, width) for m, width in kinds]
    scratch += [vmem((nz, r, 128), width) for r, width in zip(rows, WIDTH)]
    scratch += [vmem((ny, r, 128), F32) for r in rows]
    scratch += [vmem((nz, r, 128), width) for r, width in zip(rows, WIDTH)]
    scratch += [states(m, width) for m, width in kinds]
    sems = 18 + nx
    scratch += [pltpu.SemaphoreType.DMA((sems,)), pltpu.SemaphoreType.DMA((sems,)), pltpu.SemaphoreType.DMA((2,))]

    def per_device(features, weights, gains, cotangent):
        inside = pl.BlockSpec(memory_space=pltpu.VMEM)
        outside = pl.BlockSpec(memory_space=pltpu.HBM)
        shapes = (
            jax.ShapeDtypeStruct((POS, C), BF16),
            jax.ShapeDtypeStruct((POS, C), BF16),
            jax.ShapeDtypeStruct((2, TAPS * cs, C), BF16),
        )
        packed = jnp.concatenate(
            [
                features.reshape(POS, C).astype(F32),
                cotangent.reshape(POS, C).astype(F32),
                jnp.broadcast_to(gains, (8, C)),
            ]
        )
        starts, adjoints, grads = pl.pallas_call(
            functools.partial(kernel, ny, nz, nx),
            out_shape=shapes,
            in_specs=[inside, outside],
            out_specs=(inside,) * 3,
            scratch_shapes=scratch,
            compiler_params=pltpu.CompilerParams(
                collective_id=0, has_side_effects=True, vmem_limit_bytes=VMEM_BYTES
            ),
        )(
            packed,
            weights.reshape(2, TAPS, C, C),
        )
        return (
            starts.reshape(1, 1, HT, WD, C),
            adjoints.reshape(1, 1, HT, WD, C),
            grads.reshape(2, 3, 3, cs, C),
        )

    return jax.shard_map(
        per_device,
        mesh=mesh,
        in_specs=(
            P("dp", None, None, None),
            P("depth", None, None, None, None),
            P("depth", None),
            P("dp", None, None, None),
        ),
        out_specs=(
            P("depth", "dp", None, None, None),
            P("depth", "dp", None, None, None),
            P("depth", None, None, "dp", None),
        ),
        check_vma=False,
    )


def solution(mesh):
    return program(mesh, ny=4, nz=16, nx=4)
```

```python
import functools

import jax
import jax.numpy as jnp
from jax import lax
from jax.experimental import pallas as pl
from jax.experimental.pallas import tpu as pltpu
from jax.sharding import PartitionSpec as P

F32, BF16 = jnp.float32, jnp.bfloat16
STEP = 0.15
HT, WD, C = 8, 16, 256
POS = HT * WD
TAPS = 9
VMEM_BYTES = 54000 * 1024
WIDTH = (BF16, BF16, BF16, BF16)
OWNERS = (2, 1, 2, 2)


def kernel(ny, nz, nx, *refs):
    (in_ref, w_hbm, st_ref, ad_ref, gr_ref) = refs[:5]
    (wf, wt, xch, xch2, cch, g2, gz, gy) = refs[5:13]
    (buf, buf_s, us, es, dsc, at, atr, act, lhs, sg, gsend, grecv, sums) = refs[13:26]
    snds, recvs, tots, sos, sts = (refs[26 + 4 * i : 30 + 4 * i] for i in range(5))
    (send_sem, recv_sem, fetch_sem) = refs[46:]

    depth, dp = lax.axis_index("depth"), lax.axis_index("dp")
    y, z = depth // nz, depth % nz
    xx, core = dp // 2, dp % 2
    chunks = [nz // m for m in OWNERS]
    mine = [z % n for n in chunks]
    half = [2 * mine[p] // chunks[p] for p in range(4)]
    cs = C // (2 * nx)

    def at_z(k):
        return (y * nz + k, dp)

    def at_y(k):
        return (k * nz + z, dp)

    def at_x(k):
        return (depth, k * 2 + core)

    arrivals = sorted(range(1, nx), key=lambda i: min(i, nx - i))
    slot = {i: n + 1 for n, i in enumerate(arrivals)}
    sibling = (depth, xx * 2 + 1 - core)

    def over_z(body, n=nz):
        def hop(i, _):
            body((z + nz + (1 - 2 * (i % 2)) * (n // 2 - (i + 1) // 2)) % nz)
            return 0

        lax.fori_loop(0, n - 1, hop, 0)

    def over_y(body):
        for i in range(1, ny):
            body((y + i) % ny)

    def over_x(body):
        for i in reversed(arrivals):
            body(i, (xx + i) % nx)

    def send(src, dst, index, device):
        pltpu.make_async_remote_copy(
            src_ref=src,
            dst_ref=dst,
            send_sem=send_sem.at[index],
            recv_sem=recv_sem.at[index],
            device_id=device,
            device_id_type=pl.DeviceIdType.MESH,
        ).start()

    def wait(ref, sem):
        pltpu.make_async_copy(ref, ref, sem).wait()

    barrier = pltpu.get_barrier_semaphore()

    def greet(device):
        pl.semaphore_signal(barrier, inc=1, device_id=device, device_id_type=pl.DeviceIdType.MESH)

    over_z(lambda k: greet(at_z(k)))
    over_y(lambda k: greet(at_y(k)))
    over_x(lambda i, k: greet(at_x(k)))
    greet(sibling)
    fetch = [pltpu.make_async_copy(w_hbm.at[i], wf.at[i], fetch_sem.at[i]) for i in range(2)]
    for copy in fetch:
        copy.start()

    def chunked(dst, value):
        n, rows = dst.shape[0], dst.shape[1]
        for k in range(n):
            r, h = rows * (k % (n // 2)), 2 * k // n
            dst[k] = value[r : r + rows, 128 * h : 128 * h + 128].astype(dst.dtype)

    edge = jnp.zeros((WD, C), BF16)
    for b in (buf.at[0], buf.at[1], buf_s):
        for i in range(3):
            b[i, 0:WD] = edge
            b[i, POS + WD : POS + 2 * WD] = edge

    column = lax.broadcasted_iota(jnp.int32, (POS, C), 0) % WD

    def stage(b, value):
        b[0, WD : POS + WD] = jnp.where(column > 0, pltpu.roll(value, 1, 0), 0.0).astype(BF16)
        b[1, WD : POS + WD] = value.astype(BF16)
        b[2, WD : POS + WD] = jnp.where(column < WD - 1, pltpu.roll(value, POS - 1, 0), 0.0).astype(BF16)

    def conv(b, w, flip=False):
        total = None
        for t in range(TAPS):
            window = b[t % 3, WD * (t // 3) : WD * (t // 3) + POS]
            part = jnp.dot(window, w[8 - t if flip else t], preferred_element_type=F32)
            total = part if total is None else total + part
        return total

    def layer(b, u, w):
        stage(b, jnp.maximum(u, 0.0))
        return u + STEP * conv(b, w)

    def scan_order(reverse):
        return range(nz - 1, -1, -1) if reverse else range(nz)

    def offsets_out(p):
        over_z(lambda k: send(snds[p].at[k % chunks[p]], recvs[p].at[z], 3 * p, at_z(k)))

    def totals_out(p, reverse):
        wait(recvs[p].at[pl.ds(0, nz - 1)], recv_sem.at[3 * p])
        carry = None
        for k in scan_order(reverse):
            item = recvs[p][k].astype(F32)
            carry = item if carry is None else gz[k, half[p]] * carry + item
        tots[p][y] = carry.astype(tots[p].dtype)
        over_y(lambda k: send(tots[p].at[y], tots[p].at[y], 3 * p + 1, at_y(k)))

    def states_out(p, reverse, first):
        if ny > 1:
            wait(tots[p].at[pl.ds(0, ny - 1)], recv_sem.at[3 * p + 1])
        carry = first[mine[p]]
        for k in range(ny - 1, 0, -1) if reverse else range(ny - 1):
            reached = k > y if reverse else k < y
            carry = jnp.where(reached, gy[k, half[p]] * carry + tots[p][k].astype(F32), carry)
        order = scan_order(reverse)
        for k in order:
            sos[p][k] = carry.astype(sos[p].dtype)
            if k != order[-1]:
                carry = gz[k, half[p]] * carry + recvs[p][k].astype(F32)
        over_z(lambda k: send(sos[p].at[k], sts[p].at[mine[p]], 3 * p + 2, at_z(k)), chunks[p])
        sts[p][mine[p]] = sos[p][z]

    def states_in(p):
        n = chunks[p]
        wait(sts[p].at[pl.ds(0, n - 1)], recv_sem.at[3 * p + 2])
        halves = []
        for h in range(2):
            halves.append(jnp.concatenate([sts[p][h * (n // 2) + k] for k in range(n // 2)], axis=0))
        return jnp.concatenate(halves, axis=1)

    x = in_ref[0:POS]
    cot = in_ref[POS : 2 * POS]
    gain = in_ref[2 * POS : 2 * POS + 1]
    fetch[0].wait()
    middle = layer(buf.at[0], x, wf.at[0])
    for h in range(2):
        g2[h] = gain[:, 128 * h : 128 * h + 128]
    fetch[1].wait()
    chunked(snds[0], layer(buf.at[1], middle, wf.at[1]) - gain * x)
    pl.semaphore_wait(barrier, (nz - 1) + (ny - 1) + (nx - 1) + 1)
    offsets_out(0)
    over_z(lambda k: send(g2, gz.at[z], 12, at_z(k)))
    recvs[0][z] = snds[0][mine[0]]
    gz[z] = g2[...]
    chunked(xch, x)
    chunked(xch2, x)
    chunked(cch, cot)
    for i in range(2):

        def flip(t, _, i=i):
            wt[i, t] = wf[i, t].T
            return 0

        lax.fori_loop(0, TAPS, flip, 0)
    wait(gz.at[pl.ds(0, nz - 1)], recv_sem.at[12])
    product = gz[0]
    for k in range(1, nz):
        product = product * gz[k]
    gy[y] = product
    over_y(lambda k: send(gy.at[y], gy.at[y], 13, at_y(k)))
    totals_out(0, False)
    if ny > 1:
        wait(gy.at[pl.ds(0, ny - 1)], recv_sem.at[13])
    states_out(0, False, xch2)
    u1 = states_in(0).astype(F32)

    def adjoint(e):
        es[...] = e

        def one(n, _):
            stage(buf_s, (STEP * es[...]).astype(BF16).astype(F32))
            spread = conv(buf_s, wt.at[1 - n], True)
            es[...] = es[...] + jnp.where(us[1 - n] > 0.0, spread, 0.0)
            return 0

        lax.fori_loop(0, 2, one, 0)
        return es[...]

    us[0] = u1
    us[1] = layer(buf.at[0], u1, wf.at[0])
    chunked(snds[2], adjoint(cot) - gain * cot)
    offsets_out(2)
    recvs[2][z] = snds[2][mine[2]]
    u1, u2 = us[0], us[1]
    for i, u in enumerate((u1, u2)):
        active = jnp.maximum(u, 0.0)
        turned = active.T.astype(BF16)
        for k in range(nx):
            at[k, i] = turned[2 * cs * k : 2 * cs * (k + 1)]
    act[0] = active.astype(BF16)
    over_x(lambda i, k: send(at.at[k], atr.at[slot[i]], 14, at_x(k)))
    over_x(lambda i, k: send(act.at[0], act.at[slot[i]], 15, at_x(k)))
    atr[0] = at[xx]
    chunked(snds[1], layer(buf.at[1], u2, wf.at[1]) - gain * u1)
    totals_out(2, True)
    recvs[1][z] = snds[1][mine[1]]
    states_out(2, True, cch)
    offsets_out(1)
    e1 = states_in(2).astype(F32)

    d = adjoint(e1) - gain * e1
    chunked(snds[3], d)
    offsets_out(3)
    recvs[3][z] = snds[3][mine[3]]
    dsc[...] = d
    if nx > 1:
        wait(atr.at[pl.ds(0, nx - 1)], recv_sem.at[14])
        wait(act.at[pl.ds(0, nx - 1)], recv_sem.at[15])

    place = lax.broadcasted_iota(jnp.int32, (2 * cs, POS), 1)
    line, cell = place // WD, place % WD

    def windows(n, _):
        i, k = n // nx, n % nx
        value = atr[k, i].astype(F32)
        lanes = pl.ds(pl.multiple_of(POS * k, POS), POS)
        for t in range(TAPS):
            down, right = t // 3 - 1, t % 3 - 1
            moved = value
            if t != 4:
                ok = (line + down >= 0) & (line + down < HT) & (cell + right >= 0) & (cell + right < WD)
                moved = jnp.where(ok, pltpu.roll(value, (-down * WD - right) % POS, 1), 0.0)
            moved = moved.astype(BF16)
            for c in range(2):
                lhs[i, c, t, :, lanes] = moved[cs * c : cs * (c + 1)]
        return 0

    lax.fori_loop(0, 2 * nx, windows, 0)
    totals_out(1, False)
    totals_out(3, True)
    states_out(3, True, cch)
    states_out(1, False, xch)
    e2 = states_in(3).astype(F32)

    s = (STEP * e2).astype(BF16)
    sg[1, 0] = s
    over_x(lambda i, k: send(sg.at[1, 0], sg.at[1, slot[i]], 16 + slot[i], at_x(k)))

    def below(n, _):
        @pl.when(n > 0)
        def _():
            wait(sg.at[1, 0], recv_sem.at[16 + n])

        s = sg[1, n].astype(F32)
        stage(buf_s, s)
        spread = conv(buf_s, wt.at[1], True)
        sg[0, n] = (s + STEP * jnp.where(act[n].astype(F32) > 0.0, spread, 0.0)).astype(BF16)

        @pl.when(n == 0)
        def _():
            ad_ref[...] = (gain * e2 + dsc[...]).astype(BF16)

        return 0

    lax.fori_loop(0, nx, below, 0)

    def part(i, c):
        left = lhs[i, c].reshape(TAPS * cs, nx * POS)
        return jnp.dot(left, sg[i].reshape(nx * POS, C), preferred_element_type=F32)

    def parts(i, _):
        gsend[i] = part(i, 1 - core).astype(BF16)
        send(gsend.at[i], grecv.at[i], 16 + nx + i, sibling)
        sums[i] = part(i, core)
        return 0

    lax.fori_loop(0, 2, parts, 0)
    st_ref[...] = states_in(1)
    for i in range(2):
        wait(grecv.at[i], recv_sem.at[16 + nx + i])
        gr_ref[i] = (sums[i] + grecv[i].astype(F32)).astype(BF16)

    for p in range(4):
        wait(recvs[p].at[pl.ds(0, nz - 1)], send_sem.at[3 * p])
        if ny > 1:
            wait(tots[p].at[pl.ds(0, ny - 1)], send_sem.at[3 * p + 1])
        wait(sts[p].at[pl.ds(0, chunks[p] - 1)], send_sem.at[3 * p + 2])
    wait(gz.at[pl.ds(0, nz - 1)], send_sem.at[12])
    if ny > 1:
        wait(gy.at[pl.ds(0, ny - 1)], send_sem.at[13])
    if nx > 1:
        wait(atr.at[pl.ds(0, nx - 1)], send_sem.at[14])
        wait(act.at[pl.ds(0, nx - 1)], send_sem.at[15])
    for i in range(1, nx):
        wait(sg.at[1, 0], send_sem.at[16 + i])
    for i in range(2):
        wait(grecv.at[i], send_sem.at[16 + nx + i])


def program(mesh, ny, nz, nx):
    cs = C // (2 * nx)
    vmem = pltpu.VMEM

    def states(m, width):
        return vmem((nz // m, 2 * POS * m // nz, 128), width)

    scratch = [
        vmem((2, TAPS, C, C), BF16),
        vmem((2, TAPS, C, C), BF16),
        states(1, F32),
        states(2, F32),
        states(2, F32),
        vmem((2, 1, 128), F32),
        vmem((nz, 2, 1, 128), F32),
        vmem((ny, 2, 1, 128), F32),
        vmem((2, 3, POS + 2 * WD, C), BF16),
        vmem((3, POS + 2 * WD, C), BF16),
        vmem((2, POS, C), F32),
        vmem((POS, C), F32),
        vmem((POS, C), F32),
        vmem((nx, 2, 2 * cs, POS), BF16),
        vmem((nx, 2, 2 * cs, POS), BF16),
        vmem((nx, POS, C), BF16),
        vmem((2, 2, TAPS, cs, nx * POS), BF16),
        vmem((2, nx, POS, C), BF16),
        vmem((2, TAPS * cs, C), BF16),
        vmem((2, TAPS * cs, C), BF16),
        vmem((2, TAPS * cs, C), F32),
    ]
    kinds = list(zip(OWNERS, WIDTH))
    rows = [2 * POS * m // nz for m in OWNERS]
    scratch += [states(m, width) for m, width in kinds]
    scratch += [vmem((nz, r, 128), width) for r, width in zip(rows, WIDTH)]
    scratch += [vmem((ny, r, 128), width) for r, width in zip(rows, (F32, BF16, BF16, BF16))]
    back = (F32, BF16, BF16, BF16)
    scratch += [vmem((nz, r, 128), width) for r, width in zip(rows, back)]
    scratch += [states(m, width) for m, width in zip(OWNERS, back)]
    sems = 18 + nx
    scratch += [pltpu.SemaphoreType.DMA((sems,)), pltpu.SemaphoreType.DMA((sems,)), pltpu.SemaphoreType.DMA((2,))]

    def per_device(features, weights, gains, cotangent):
        inside = pl.BlockSpec(memory_space=pltpu.VMEM)
        outside = pl.BlockSpec(memory_space=pltpu.HBM)
        shapes = (
            jax.ShapeDtypeStruct((POS, C), BF16),
            jax.ShapeDtypeStruct((POS, C), BF16),
            jax.ShapeDtypeStruct((2, TAPS * cs, C), BF16),
        )
        packed = jnp.concatenate(
            [
                features.reshape(POS, C).astype(F32),
                cotangent.reshape(POS, C).astype(F32),
                jnp.broadcast_to(gains, (8, C)),
            ]
        )
        starts, adjoints, grads = pl.pallas_call(
            functools.partial(kernel, ny, nz, nx),
            out_shape=shapes,
            in_specs=[inside, outside],
            out_specs=(inside,) * 3,
            scratch_shapes=scratch,
            compiler_params=pltpu.CompilerParams(
                collective_id=0, has_side_effects=True, vmem_limit_bytes=VMEM_BYTES
            ),
        )(
            packed,
            weights.reshape(2, TAPS, C, C),
        )
        return (
            starts.reshape(1, 1, HT, WD, C),
            adjoints.reshape(1, 1, HT, WD, C),
            grads.reshape(2, 3, 3, cs, C),
        )

    return jax.shard_map(
        per_device,
        mesh=mesh,
        in_specs=(
            P("dp", None, None, None),
            P("depth", None, None, None, None),
            P("depth", None),
            P("dp", None, None, None),
        ),
        out_specs=(
            P("depth", "dp", None, None, None),
            P("depth", "dp", None, None, None),
            P("depth", None, None, "dp", None),
        ),
        check_vma=False,
    )


def solution(mesh):
    return program(mesh, ny=4, nz=16, nx=4)
```

```python
import functools

import jax
import jax.numpy as jnp
from jax import lax
from jax.experimental import pallas as pl
from jax.experimental.pallas import tpu as pltpu
from jax.sharding import PartitionSpec as P

F32, BF16 = jnp.float32, jnp.bfloat16
STEP = 0.15
HT, WD, C = 8, 16, 256
POS = HT * WD
TAPS = 9
VMEM_BYTES = 54000 * 1024
WIDTH = (BF16, BF16, BF16, BF16)
OWNERS = (2, 1, 2, 2)


def kernel(ny, nz, nx, *refs):
    (in_ref, w_hbm, st_ref, ad_ref, gr_ref) = refs[:5]
    (wf, wt, xch, zeros, cch, g2, gz, gy) = refs[5:13]
    (buf, buf_s, us, es, dsc, at, atr, act, lhs, sg, gsend, grecv, sums) = refs[13:26]
    snds, recvs, tots, sos, sts = (refs[26 + 4 * i : 30 + 4 * i] for i in range(5))
    (send_sem, recv_sem, fetch_sem) = refs[46:]

    depth, dp = lax.axis_index("depth"), lax.axis_index("dp")
    y, z = depth // nz, depth % nz
    xx, core = dp // 2, dp % 2
    chunks = [nz // m for m in OWNERS]
    mine = [z % n for n in chunks]
    half = [2 * mine[p] // chunks[p] for p in range(4)]
    cs = C // (2 * nx)

    def at_z(k):
        return (y * nz + k, dp)

    def at_y(k):
        return (k * nz + z, dp)

    def at_x(k):
        return (depth, k * 2 + core)

    arrivals = sorted(range(1, nx), key=lambda i: min(i, nx - i))
    slot = {i: n + 1 for n, i in enumerate(arrivals)}
    sibling = (depth, xx * 2 + 1 - core)

    def over_z(body, n=nz):
        def hop(i, _):
            body((z + nz + (1 - 2 * (i % 2)) * (n // 2 - (i + 1) // 2)) % nz)
            return 0

        lax.fori_loop(0, n - 1, hop, 0)

    def over_y(body):
        for i in range(1, ny):
            body((y + i) % ny)

    def over_x(body):
        for i in reversed(arrivals):
            body(i, (xx + i) % nx)

    def send(src, dst, index, device):
        pltpu.make_async_remote_copy(
            src_ref=src,
            dst_ref=dst,
            send_sem=send_sem.at[index],
            recv_sem=recv_sem.at[index],
            device_id=device,
            device_id_type=pl.DeviceIdType.MESH,
        ).start()

    def wait(ref, sem):
        pltpu.make_async_copy(ref, ref, sem).wait()

    barrier = pltpu.get_barrier_semaphore()

    def greet(device):
        pl.semaphore_signal(barrier, inc=1, device_id=device, device_id_type=pl.DeviceIdType.MESH)

    over_z(lambda k: greet(at_z(k)))
    over_y(lambda k: greet(at_y(k)))
    over_x(lambda i, k: greet(at_x(k)))
    greet(sibling)
    fetch = [pltpu.make_async_copy(w_hbm.at[i], wf.at[i], fetch_sem.at[i]) for i in range(2)]
    for copy in fetch:
        copy.start()

    def chunked(dst, value):
        n, rows = dst.shape[0], dst.shape[1]
        for k in range(n):
            r, h = rows * (k % (n // 2)), 2 * k // n
            dst[k] = value[r : r + rows, 128 * h : 128 * h + 128].astype(dst.dtype)

    edge = jnp.zeros((WD, C), BF16)
    for b in (buf.at[0], buf.at[1], buf_s):
        for i in range(3):
            b[i, 0:WD] = edge
            b[i, POS + WD : POS + 2 * WD] = edge

    column = lax.broadcasted_iota(jnp.int32, (POS, C), 0) % WD

    def stage(b, value):
        b[0, WD : POS + WD] = jnp.where(column > 0, pltpu.roll(value, 1, 0), 0.0).astype(BF16)
        b[1, WD : POS + WD] = value.astype(BF16)
        b[2, WD : POS + WD] = jnp.where(column < WD - 1, pltpu.roll(value, POS - 1, 0), 0.0).astype(BF16)

    def conv(b, w, flip=False):
        total = None
        for t in range(TAPS):
            window = b[t % 3, WD * (t // 3) : WD * (t // 3) + POS]
            part = jnp.dot(window, w[8 - t if flip else t], preferred_element_type=F32)
            total = part if total is None else total + part
        return total

    def layer(b, u, w):
        stage(b, jnp.maximum(u, 0.0))
        return u + STEP * conv(b, w)

    def scan_order(reverse):
        return range(nz - 1, -1, -1) if reverse else range(nz)

    def offsets_out(p):
        over_z(lambda k: send(snds[p].at[k % chunks[p]], recvs[p].at[z], 3 * p, at_z(k)))

    def totals_out(p, reverse):
        wait(recvs[p].at[pl.ds(0, nz - 1)], recv_sem.at[3 * p])
        carry = None
        for k in scan_order(reverse):
            item = recvs[p][k].astype(F32)
            carry = item if carry is None else gz[k, half[p]] * carry + item
        tots[p][y] = carry.astype(tots[p].dtype)
        over_y(lambda k: send(tots[p].at[y], tots[p].at[y], 3 * p + 1, at_y(k)))

    def states_out(p, reverse, first):
        if ny > 1:
            wait(tots[p].at[pl.ds(0, ny - 1)], recv_sem.at[3 * p + 1])
        carry = first[mine[p]]
        for k in range(ny - 1, 0, -1) if reverse else range(ny - 1):
            reached = k > y if reverse else k < y
            carry = jnp.where(reached, gy[k, half[p]] * carry + tots[p][k].astype(F32), carry)
        order = scan_order(reverse)
        for k in order:
            sos[p][k] = carry.astype(sos[p].dtype)
            if k != order[-1]:
                carry = gz[k, half[p]] * carry + recvs[p][k].astype(F32)
        over_z(lambda k: send(sos[p].at[k], sts[p].at[mine[p]], 3 * p + 2, at_z(k)), chunks[p])
        sts[p][mine[p]] = sos[p][z]

    def states_in(p):
        n = chunks[p]
        wait(sts[p].at[pl.ds(0, n - 1)], recv_sem.at[3 * p + 2])
        halves = []
        for h in range(2):
            halves.append(jnp.concatenate([sts[p][h * (n // 2) + k] for k in range(n // 2)], axis=0))
        return jnp.concatenate(halves, axis=1)

    x = in_ref[0:POS]
    cot = in_ref[POS : 2 * POS]
    gain = in_ref[2 * POS : 2 * POS + 1]
    fetch[0].wait()
    middle = layer(buf.at[0], x, wf.at[0])
    for h in range(2):
        g2[h] = gain[:, 128 * h : 128 * h + 128]
    fetch[1].wait()
    chunked(snds[0], layer(buf.at[1], middle, wf.at[1]) - gain * x)
    pl.semaphore_wait(barrier, (nz - 1) + (ny - 1) + (nx - 1) + 1)
    offsets_out(0)
    over_z(lambda k: send(g2, gz.at[z], 12, at_z(k)))
    recvs[0][z] = snds[0][mine[0]]
    gz[z] = g2[...]
    chunked(xch, x)
    zeros[...] = jnp.zeros_like(zeros)
    chunked(cch, cot)
    for i in range(2):

        def flip(t, _, i=i):
            wt[i, t] = wf[i, t].T
            return 0

        lax.fori_loop(0, TAPS, flip, 0)
    wait(gz.at[pl.ds(0, nz - 1)], recv_sem.at[12])
    product = gz[0]
    for k in range(1, nz):
        product = product * gz[k]
    gy[y] = product
    over_y(lambda k: send(gy.at[y], gy.at[y], 13, at_y(k)))
    totals_out(0, False)
    if ny > 1:
        wait(gy.at[pl.ds(0, ny - 1)], recv_sem.at[13])
    states_out(0, False, zeros)
    factor = jnp.ones((2, 1, 128), F32)
    for k in range(ny - 1):
        factor = jnp.where(k < y, factor * gy[k], factor)
    for k in range(nz - 1):
        factor = jnp.where(k < z, factor * gz[k], factor)
    factor = jnp.concatenate([factor[0], factor[1]], axis=1)
    u1 = states_in(0).astype(F32) + factor * x

    def adjoint(e):
        es[...] = e

        def one(n, _):
            stage(buf_s, (STEP * es[...]).astype(BF16).astype(F32))
            spread = conv(buf_s, wt.at[1 - n], True)
            es[...] = es[...] + jnp.where(us[1 - n] > 0.0, spread, 0.0)
            return 0

        lax.fori_loop(0, 2, one, 0)
        return es[...]

    us[0] = u1
    us[1] = layer(buf.at[0], u1, wf.at[0])
    chunked(snds[2], adjoint(cot) - gain * cot)
    offsets_out(2)
    recvs[2][z] = snds[2][mine[2]]
    u1, u2 = us[0], us[1]
    for i, u in enumerate((u1, u2)):
        active = jnp.maximum(u, 0.0)
        turned = active.T.astype(BF16)
        for k in range(nx):
            at[k, i] = turned[2 * cs * k : 2 * cs * (k + 1)]
    act[0] = active.astype(BF16)
    over_x(lambda i, k: send(at.at[k], atr.at[slot[i]], 14, at_x(k)))
    over_x(lambda i, k: send(act.at[0], act.at[slot[i]], 15, at_x(k)))
    atr[0] = at[xx]
    chunked(snds[1], layer(buf.at[1], u2, wf.at[1]) - gain * u1)
    totals_out(2, True)
    recvs[1][z] = snds[1][mine[1]]
    states_out(2, True, cch)
    offsets_out(1)
    e1 = states_in(2).astype(F32)

    d = adjoint(e1) - gain * e1
    chunked(snds[3], d)
    offsets_out(3)
    recvs[3][z] = snds[3][mine[3]]
    dsc[...] = d
    if nx > 1:
        wait(atr.at[pl.ds(0, nx - 1)], recv_sem.at[14])
        wait(act.at[pl.ds(0, nx - 1)], recv_sem.at[15])

    place = lax.broadcasted_iota(jnp.int32, (2 * cs, POS), 1)
    line, cell = place // WD, place % WD

    def windows(n, _):
        i, k = n // nx, n % nx
        value = atr[k, i].astype(F32)
        lanes = pl.ds(pl.multiple_of(POS * k, POS), POS)
        for t in range(TAPS):
            down, right = t // 3 - 1, t % 3 - 1
            moved = value
            if t != 4:
                ok = (line + down >= 0) & (line + down < HT) & (cell + right >= 0) & (cell + right < WD)
                moved = jnp.where(ok, pltpu.roll(value, (-down * WD - right) % POS, 1), 0.0)
            moved = moved.astype(BF16)
            for c in range(2):
                lhs[i, c, t, :, lanes] = moved[cs * c : cs * (c + 1)]
        return 0

    lax.fori_loop(0, 2 * nx, windows, 0)
    totals_out(1, False)
    totals_out(3, True)
    states_out(3, True, cch)
    states_out(1, False, xch)
    e2 = states_in(3).astype(F32)

    s = (STEP * e2).astype(BF16)
    sg[1, 0] = s
    over_x(lambda i, k: send(sg.at[1, 0], sg.at[1, slot[i]], 16 + slot[i], at_x(k)))

    def below(n, _):
        @pl.when(n > 0)
        def _():
            wait(sg.at[1, 0], recv_sem.at[16 + n])

        s = sg[1, n].astype(F32)
        stage(buf_s, s)
        spread = conv(buf_s, wt.at[1], True)
        sg[0, n] = (s + STEP * jnp.where(act[n].astype(F32) > 0.0, spread, 0.0)).astype(BF16)

        @pl.when(n == 0)
        def _():
            ad_ref[...] = (gain * e2 + dsc[...]).astype(BF16)

        return 0

    lax.fori_loop(0, nx, below, 0)

    def part(i, c):
        left = lhs[i, c].reshape(TAPS * cs, nx * POS)
        return jnp.dot(left, sg[i].reshape(nx * POS, C), preferred_element_type=F32)

    def parts(i, _):
        gsend[i] = part(i, 1 - core).astype(BF16)
        send(gsend.at[i], grecv.at[i], 16 + nx + i, sibling)
        sums[i] = part(i, core)
        return 0

    lax.fori_loop(0, 2, parts, 0)
    st_ref[...] = states_in(1)
    for i in range(2):
        wait(grecv.at[i], recv_sem.at[16 + nx + i])
        gr_ref[i] = (sums[i] + grecv[i].astype(F32)).astype(BF16)

    for p in range(4):
        wait(recvs[p].at[pl.ds(0, nz - 1)], send_sem.at[3 * p])
        if ny > 1:
            wait(tots[p].at[pl.ds(0, ny - 1)], send_sem.at[3 * p + 1])
        wait(sts[p].at[pl.ds(0, chunks[p] - 1)], send_sem.at[3 * p + 2])
    wait(gz.at[pl.ds(0, nz - 1)], send_sem.at[12])
    if ny > 1:
        wait(gy.at[pl.ds(0, ny - 1)], send_sem.at[13])
    if nx > 1:
        wait(atr.at[pl.ds(0, nx - 1)], send_sem.at[14])
        wait(act.at[pl.ds(0, nx - 1)], send_sem.at[15])
    for i in range(1, nx):
        wait(sg.at[1, 0], send_sem.at[16 + i])
    for i in range(2):
        wait(grecv.at[i], send_sem.at[16 + nx + i])


def program(mesh, ny, nz, nx):
    cs = C // (2 * nx)
    vmem = pltpu.VMEM

    def states(m, width):
        return vmem((nz // m, 2 * POS * m // nz, 128), width)

    scratch = [
        vmem((2, TAPS, C, C), BF16),
        vmem((2, TAPS, C, C), BF16),
        states(1, F32),
        states(2, F32),
        states(2, F32),
        vmem((2, 1, 128), F32),
        vmem((nz, 2, 1, 128), F32),
        vmem((ny, 2, 1, 128), F32),
        vmem((2, 3, POS + 2 * WD, C), BF16),
        vmem((3, POS + 2 * WD, C), BF16),
        vmem((2, POS, C), F32),
        vmem((POS, C), F32),
        vmem((POS, C), F32),
        vmem((nx, 2, 2 * cs, POS), BF16),
        vmem((nx, 2, 2 * cs, POS), BF16),
        vmem((nx, POS, C), BF16),
        vmem((2, 2, TAPS, cs, nx * POS), BF16),
        vmem((2, nx, POS, C), BF16),
        vmem((2, TAPS * cs, C), BF16),
        vmem((2, TAPS * cs, C), BF16),
        vmem((2, TAPS * cs, C), F32),
    ]
    kinds = list(zip(OWNERS, WIDTH))
    rows = [2 * POS * m // nz for m in OWNERS]
    scratch += [states(m, width) for m, width in kinds]
    scratch += [vmem((nz, r, 128), width) for r, width in zip(rows, WIDTH)]
    scratch += [vmem((ny, r, 128), width) for r, width in zip(rows, (F32, BF16, BF16, BF16))]
    back = (F32, BF16, BF16, BF16)
    scratch += [vmem((nz, r, 128), width) for r, width in zip(rows, back)]
    scratch += [states(m, width) for m, width in zip(OWNERS, back)]
    sems = 18 + nx
    scratch += [pltpu.SemaphoreType.DMA((sems,)), pltpu.SemaphoreType.DMA((sems,)), pltpu.SemaphoreType.DMA((2,))]

    def per_device(features, weights, gains, cotangent):
        inside = pl.BlockSpec(memory_space=pltpu.VMEM)
        outside = pl.BlockSpec(memory_space=pltpu.HBM)
        shapes = (
            jax.ShapeDtypeStruct((POS, C), BF16),
            jax.ShapeDtypeStruct((POS, C), BF16),
            jax.ShapeDtypeStruct((2, TAPS * cs, C), BF16),
        )
        packed = jnp.concatenate(
            [
                features.reshape(POS, C).astype(F32),
                cotangent.reshape(POS, C).astype(F32),
                jnp.broadcast_to(gains, (8, C)),
            ]
        )
        starts, adjoints, grads = pl.pallas_call(
            functools.partial(kernel, ny, nz, nx),
            out_shape=shapes,
            in_specs=[inside, outside],
            out_specs=(inside,) * 3,
            scratch_shapes=scratch,
            compiler_params=pltpu.CompilerParams(
                collective_id=0, has_side_effects=True, vmem_limit_bytes=VMEM_BYTES
            ),
        )(
            packed,
            weights.reshape(2, TAPS, C, C),
        )
        return (
            starts.reshape(1, 1, HT, WD, C),
            adjoints.reshape(1, 1, HT, WD, C),
            grads.reshape(2, 3, 3, cs, C),
        )

    return jax.shard_map(
        per_device,
        mesh=mesh,
        in_specs=(
            P("dp", None, None, None),
            P("depth", None, None, None, None),
            P("depth", None),
            P("dp", None, None, None),
        ),
        out_specs=(
            P("depth", "dp", None, None, None),
            P("depth", "dp", None, None, None),
            P("depth", None, None, "dp", None),
        ),
        check_vma=False,
    )


def solution(mesh):
    return program(mesh, ny=4, nz=16, nx=4)
```
